32 devices in a mesh: section: 2 (over core), expert: 16 (over z, y, x).
Axes of the slice: x: 2, y: 2, z: 4, core: 2. Of those that a mesh axis runs over, the one named last changes fastest.
Arguments:
- grad_out: bfloat16 [2, 2048, 3584], P('section', 'expert'), may hold values from -6 to 6
- expert_ids: int32 [2, 2048, 8], P('section', 'expert'), may hold values from 0 to 15, all different within a row; in each aligned block of 128 rows (0 to 127, 128 to 255, ..., all dimensions but the last counted through in order) at most 80 rows name the same one
- gate_weights: bfloat16 [2, 2048, 8], P('section', 'expert'), may hold values from 0.019897461 to 0.5
- down_weight: bfloat16 [2, 16, 1024, 3584], P('section', 'expert'), may hold values from -0.09375 to 0.09375
- hidden_saved: bfloat16 [2, 16, 16, 80, 1024], P('section', 'expert'), may hold values from -0.19921875 to 0.19921875
Outputs:
- hidden_grad: bfloat16 [2, 16, 16, 80, 1024], P('section', 'expert')
- gate_grad: float32 [2, 2048, 8], P('section', 'expert')
The draws below stay inside these ranges and needn't reach their ends.
Inputs may be any that keep to these rules, and one draw needn't show every extreme that they name: `expert_ids`: each token names 8 distinct experts; among the tokens of one index of expert in one section, no expert is named by more than 80 of them, a bound that some block reaches.
All inputs are finite; a program needn't handle non-finite values.
Results may differ from the reference program's by a relative error of at most 0.001.
Values may be sent and summed in bfloat16 or wider, within the bound.
A program may use at most 128 MiB of HBM per device.

```python
import math
import jax
import jax.numpy as jnp
import numpy as np
from jax import lax

D = 3584
HID = 1024
TOP = 8
TOK_DEV = 128
SECTIONS = 2
EXPERTS = 16
TOKENS = 2048
MOST = 80
N_EXPERT = 16


def level_of(rng, dims, pieces, smallest, largest):
    level = 1.0
    for axis_at, blocks in pieces:
        heights = jax.random.uniform(jax.random.fold_in(jax.random.fold_in(rng, 6), axis_at), (blocks,), jnp.float32, smallest / len(pieces), largest / len(pieces))
        level = level * jnp.repeat(jnp.exp(heights), dims[axis_at] // blocks).reshape((-1,) + (1,) * (len(dims) - 1 - axis_at))
    return level


def routed_block(key, own, number, rows, number_of, top, most, lean):
    ranking = jax.random.permutation(key, number_of)
    crowded, usual = shares(number_of, rows * top, most, lean, True), shares(number_of, rows * top, most, lean, False)
    places = jnp.arange(number_of)

    def named(sizes, offset_by):
        used = int((sizes > 0).sum())
        fixed = max(1, used // 4)
        moved = fixed + (places - fixed + offset_by * (used - fixed)) % max(1, number_of - fixed)
        return jnp.zeros((number_of,), jnp.int32).at[ranking[jnp.where(places < fixed, places, moved)]].set(jnp.asarray(sizes, jnp.int32))

    sizes = jnp.where(number % 4 == 0, named(crowded, number // 4), named(usual, number - number // 4 - 1))
    mixed = jax.random.permutation(jax.random.fold_in(own, 3), number_of)
    giver, receiver = mixed[0:number_of // 2 * 2:2], mixed[1:number_of // 2 * 2:2]
    slack = jnp.minimum(sizes[giver] - 1, most - sizes[receiver]) // 2
    slack = jnp.where((giver == ranking[0]) | (receiver == ranking[0]) | (sizes[receiver] == 0), 0, jnp.maximum(slack, 0))
    moved = jax.random.randint(jax.random.fold_in(own, 4), (number_of // 2,), 0, 1 << 20) % (slack + 1)
    sizes = sizes.at[giver].add(-moved).at[receiver].add(moved)
    items = jnp.searchsorted(jnp.cumsum(sizes), jnp.arange(rows * top), side="right").astype(jnp.int32)
    table = items.reshape(top, rows).T
    table = table[jax.random.permutation(jax.random.fold_in(own, 1), rows)]
    offset_by = jax.random.randint(jax.random.fold_in(own, 2), (rows, 1), 0, top)
    return jnp.take_along_axis(table, (jnp.arange(top)[None, :] + offset_by) % top, axis=1)


def shares(number_of, total, reach, lean, full):
    loads = [(1 << 20) // math.isqrt(grade ** lean) + 1 for grade in range(1, number_of + 1)]
    largest = reach if full else min(reach, max(-(-total // number_of), total * loads[0] // sum(loads)))
    least = 1 if total - largest >= number_of - 1 else 0
    counts, spare = [largest] + [least] * (number_of - 1), total - largest - least * (number_of - 1)
    while spare > 0:
        candidates = [i for i in range(1, number_of) if counts[i] < largest] or [i for i in range(1, number_of) if counts[i] < reach]
        mass, budget = sum([loads[i] for i in candidates]), spare
        for i in candidates:
            addition = min(reach - counts[i], max(1, budget * loads[i] // mass), spare)
            counts[i] = counts[i] + addition
            spare = spare - addition
    return np.array(counts)


def bell_draw(stream_key, dims, spread, limit, split=(), kind=jnp.bfloat16):
    entries = spread * jax.random.normal(stream_key, dims, jnp.float32)
    if split:
        entries = entries * level_of(stream_key, dims, split, -0.22, 0.18)
    return jnp.clip(entries, -limit, limit).astype(kind)


def setup_inputs(seed: int = 0) -> dict:
    splits = jax.random.split(jax.random.key(seed), 6)
    grad_out = bell_draw(splits[0], (SECTIONS, TOKENS, D), 1.0, 6.0, ((0, 2), (1, 16)))
    expert_ids_keys = jax.random.split(jax.random.fold_in(splits[1], 1), SECTIONS * TOKENS // TOK_DEV)
    expert_ids_turns = jax.random.permutation(jax.random.fold_in(splits[1], 3), SECTIONS * TOKENS // TOK_DEV)
    expert_ids = jax.vmap(lambda own, number: routed_block(jax.random.fold_in(splits[1], 2), own, number, TOK_DEV, EXPERTS, TOP, MOST, 2))(expert_ids_keys, expert_ids_turns).reshape((SECTIONS, TOKENS, TOP))
    gate_weights = jnp.clip(jnp.exp(math.log(0.5) - 3.224016 * jax.random.uniform(splits[2], (SECTIONS, TOKENS, TOP), jnp.float32) ** level_of(splits[2], (SECTIONS, TOKENS, TOP), ((0, 2), (1, 16)), -0.2, 0.2)), 0.019897461, 0.5).astype(jnp.bfloat16)
    down_weight = bell_draw(splits[3], (SECTIONS, EXPERTS, HID, D), D ** -0.5, 0.09375, ((0, 2), (1, 16)))
    hidden_saved = bell_draw(splits[4], (SECTIONS, EXPERTS, N_EXPERT, MOST, HID), 0.03125, 0.19921875, ((0, 2), (1, 16)))
    return dict(grad_out=grad_out, expert_ids=expert_ids, gate_weights=gate_weights, down_weight=down_weight, hidden_saved=hidden_saved)


def slot_ranks(ids_block):
    flat = ids_block.reshape(-1).astype(jnp.int32)
    onehot = (flat[:, None] == jnp.arange(EXPERTS, dtype=jnp.int32)[None, :]).astype(jnp.int32)
    rank = jnp.sum(jnp.cumsum(onehot, 0) * onehot, 1) - 1
    return flat, rank.astype(jnp.int32)


def reference(grad_out, expert_ids, gate_weights, down_weight, hidden_saved):
    incoming = jnp.roll(grad_out, -1, axis=0)
    slots = TOK_DEV * TOP
    total = EXPERTS * N_EXPERT * MOST
    grads_all = []
    gates_all = []
    for section_num in range(SECTIONS):
        flat, rank = jax.vmap(slot_ranks)(expert_ids[section_num].reshape(N_EXPERT, TOK_DEV, TOP))
        source = jnp.arange(N_EXPERT, dtype=jnp.int32)[:, None]
        token = source * TOK_DEV + (jnp.arange(slots, dtype=jnp.int32) // TOP)[None, :]
        dest = ((flat * N_EXPERT + source) * MOST + rank).reshape(-1)
        token_of = jnp.zeros((total,), jnp.int32).at[dest].set(token.reshape(-1))
        weight_of = jnp.zeros((total,), jnp.bfloat16).at[dest].set(gate_weights[section_num].reshape(-1))
        live_of = jnp.zeros((total,), jnp.bool_).at[dest].set(True)
        section_grad = incoming[section_num]
        section_down = down_weight[section_num]
        section_hidden = hidden_saved[section_num]

        def per_expert(expert_num):
            start = expert_num * (N_EXPERT * MOST)
            index = lax.dynamic_slice_in_dim(token_of, start, N_EXPERT * MOST)
            live = lax.dynamic_slice_in_dim(live_of, start, N_EXPERT * MOST)
            weight = lax.dynamic_slice_in_dim(weight_of, start, N_EXPERT * MOST)
            rows = jnp.where(live[:, None], section_grad[index], jnp.zeros((), jnp.bfloat16))
            back = lax.dot_general(rows, section_down[expert_num], (((1,), (1,)), ((), ())), preferred_element_type=jnp.float32)
            hidden_grad = (weight.astype(jnp.float32)[:, None] * back).astype(jnp.bfloat16)
            saved = section_hidden[expert_num].reshape(N_EXPERT * MOST, HID).astype(jnp.float32)
            slot_grad = jnp.sum(saved * back, axis=1)
            return hidden_grad.reshape(N_EXPERT, MOST, HID), slot_grad

        grads, slot_grads = lax.map(per_expert, jnp.arange(EXPERTS, dtype=jnp.int32))
        grads_all.append(grads)
        gates_all.append(slot_grads.reshape(-1)[dest].reshape(TOKENS, TOP))
    return jnp.stack(grads_all), jnp.stack(gates_all)
```

```python
import jax
import jax.numpy as jnp
from jax import lax
from jax.sharding import PartitionSpec as P


def shifted(x, axis, by):
    size = lax.axis_size(axis)
    return lax.ppermute(x, axis, [(i, (i + by) % size) for i in range(size)])


def slot_places(ids_local, experts, most):
    flat = ids_local.reshape(-1)
    onehot = (flat[:, None] == jnp.arange(experts, dtype=jnp.int32)[None, :]).astype(jnp.int32)
    rank = jnp.sum(jnp.cumsum(onehot, 0) * onehot, 1) - 1
    return flat * most + rank


def pack_rows(grad_local, dest, experts, most, top_count):
    token = jnp.arange(dest.shape[0], dtype=jnp.int32) // top_count
    rows = (
        jnp.zeros((experts * most, grad_local.shape[1]), jnp.bfloat16)
        .at[dest]
        .set(grad_local[token])
    )
    return rows.reshape(experts, most, grad_local.shape[1])


def pack_gates(gates_local, dest, experts, most):
    weights = jnp.zeros((experts * most,), jnp.bfloat16).at[dest].set(gates_local.reshape(-1))
    return weights.reshape(experts, most)


def project_back(rows_in, weight_part):
    flat_rows = rows_in.reshape(-1, rows_in.shape[2])
    return lax.dot_general(
        flat_rows, weight_part, (((1,), (1,)), ((), ())), preferred_element_type=jnp.float32
    )


def local(grad_out, expert_ids, gate_weights, down_weight, hidden_saved):
    experts = lax.axis_size("expert")
    most = hidden_saved.shape[3]
    width = grad_out.shape[2]
    hidden_width = down_weight.shape[2]
    top_count = expert_ids.shape[2]
    dest = slot_places(expert_ids[0], experts, most)
    gate_buf = pack_gates(gate_weights[0], dest, experts, most)
    half = width // 2
    lower = shifted(grad_out[0][:, :half], "section", -1)
    lower_buf = pack_rows(lower, dest, experts, most, top_count)
    lower_in, gates_in = (
        lax.all_to_all(lower_buf, "expert", split_axis=0, concat_axis=0, tiled=True),
        lax.all_to_all(gate_buf, "expert", split_axis=0, concat_axis=0, tiled=True),
    )
    upper = shifted(grad_out[0][:, half:], "section", -1)
    upper_buf = pack_rows(upper, dest, experts, most, top_count)
    upper_in = lax.all_to_all(upper_buf, "expert", split_axis=0, concat_axis=0, tiled=True)
    back = project_back(lower_in, down_weight[0, 0][:, :half]) + project_back(
        upper_in, down_weight[0, 0][:, half:]
    )
    hidden_grad = (gates_in.reshape(-1).astype(jnp.float32)[:, None] * back).astype(jnp.bfloat16)
    saved = hidden_saved[0, 0].reshape(experts * most, hidden_width)
    slot_grad = jnp.sum(saved.astype(jnp.float32) * back, axis=1).reshape(experts, most)
    returned = lax.all_to_all(slot_grad, "expert", split_axis=0, concat_axis=0, tiled=True)
    gate_grad = returned.reshape(-1)[dest].reshape(1, expert_ids.shape[1], top_count)
    return (hidden_grad.reshape(1, 1, experts, most, hidden_width), gate_grad)


def gathered(grad_out, expert_ids, gate_weights, down_weight, hidden_saved):
    experts = lax.axis_size("expert")
    most = hidden_saved.shape[3]
    width = grad_out.shape[2]
    tokens = grad_out.shape[1]
    hidden_width = down_weight.shape[2]
    me = lax.axis_index("expert")
    ids = lax.all_gather(expert_ids[0], "expert", axis=0)
    gates = lax.all_gather(gate_weights[0], "expert", axis=0)
    incoming = shifted(grad_out[0], "section", -1)
    grads = lax.all_gather(incoming, "expert", axis=0)
    named = ids == me
    owned = jnp.any(named, axis=2)
    place = jnp.arange(tokens, dtype=jnp.int32)
    earlier = (place[:, None] < place[None, :]).astype(jnp.bfloat16)
    before = jnp.dot(owned.astype(jnp.bfloat16), earlier, preferred_element_type=jnp.float32)
    rank = jnp.where(owned, before.astype(jnp.int32), -1)
    gate = jnp.sum(jnp.where(named, gates.astype(jnp.float32), 0.0), axis=2)
    select = rank[:, None, :] == jnp.arange(most, dtype=jnp.int32)[None, :, None]
    rows = lax.dot_general(
        select.astype(jnp.bfloat16), grads, (((2,), (1,)), ((0,), (0,))), preferred_element_type=jnp.bfloat16
    )
    back = project_back(rows, down_weight[0, 0]).reshape(experts, most, hidden_width)
    weight = jnp.sum(jnp.where(select, gate[:, None, :], 0.0), axis=2)
    hidden_grad = (weight[:, :, None] * back).astype(jnp.bfloat16)
    slot_grad = jnp.sum(hidden_saved[0, 0].astype(jnp.float32) * back, axis=2)
    by_token = jnp.sum(jnp.where(select, slot_grad[:, :, None], 0.0), axis=1)
    returned = lax.all_to_all(by_token, "expert", split_axis=0, concat_axis=0, tiled=True)
    mine = expert_ids[0][:, :, None] == jnp.arange(experts, dtype=jnp.int32)
    gate_grad = jnp.sum(jnp.where(mine, returned.T[:, None, :], 0.0), axis=2)
    return hidden_grad[None, None], gate_grad[None]


def solution(mesh):
    in_specs = (
        P("section", "expert", None),
        P("section", "expert", None),
        P("section", "expert", None),
        P("section", "expert", None, None),
        P("section", "expert", None, None, None),
    )
    out_specs = (P("section", "expert", None, None, None), P("section", "expert", None))
    return jax.shard_map(gathered, mesh=mesh, in_specs=in_specs, out_specs=out_specs, check_vma=False)
```

```python
import functools

import jax
import jax.numpy as jnp
from jax import lax
from jax.experimental import pallas as pl
from jax.experimental.pallas import tpu as pltpu
from jax.sharding import PartitionSpec as P

MESH = pl.DeviceIdType.MESH
DEPTH, BATCH = 4, 4


def shifted(x, axis, by):
    size = lax.axis_size(axis)
    return lax.ppermute(x, axis, [(i, (i + by) % size) for i in range(size)])


def project_back(rows_in, weight_part):
    flat_rows = rows_in.reshape(-1, rows_in.shape[2])
    return lax.dot_general(
        flat_rows, weight_part, (((1,), (1,)), ((), ())), preferred_element_type=jnp.float32
    )


def gathered(grad_out, expert_ids, gate_weights, down_weight, hidden_saved):
    experts = lax.axis_size("expert")
    most = hidden_saved.shape[3]
    width = grad_out.shape[2]
    tokens = grad_out.shape[1]
    hidden_width = down_weight.shape[2]
    me = lax.axis_index("expert")
    ids = lax.all_gather(expert_ids[0], "expert", axis=0)
    gates = lax.all_gather(gate_weights[0], "expert", axis=0)
    incoming = shifted(grad_out[0], "section", -1)
    grads = lax.all_gather(incoming, "expert", axis=0)
    named = ids == me
    owned = jnp.any(named, axis=2)
    place = jnp.arange(tokens, dtype=jnp.int32)
    earlier = (place[:, None] < place[None, :]).astype(jnp.bfloat16)
    before = jnp.dot(owned.astype(jnp.bfloat16), earlier, preferred_element_type=jnp.float32)
    rank = jnp.where(owned, before.astype(jnp.int32), -1)
    gate = jnp.sum(jnp.where(named, gates.astype(jnp.float32), 0.0), axis=2)
    select = rank[:, None, :] == jnp.arange(most, dtype=jnp.int32)[None, :, None]
    rows = lax.dot_general(
        select.astype(jnp.bfloat16), grads, (((2,), (1,)), ((0,), (0,))), preferred_element_type=jnp.bfloat16
    )
    back = project_back(rows, down_weight[0, 0]).reshape(experts, most, hidden_width)
    weight = jnp.sum(jnp.where(select, gate[:, None, :], 0.0), axis=2)
    hidden_grad = (weight[:, :, None] * back).astype(jnp.bfloat16)
    slot_grad = jnp.sum(hidden_saved[0, 0].astype(jnp.float32) * back, axis=2)
    by_token = jnp.sum(jnp.where(select, slot_grad[:, :, None], 0.0), axis=1)
    returned = lax.all_to_all(by_token, "expert", split_axis=0, concat_axis=0, tiled=True)
    mine = expert_ids[0][:, :, None] == jnp.arange(experts, dtype=jnp.int32)
    gate_grad = jnp.sum(jnp.where(mine, returned.T[:, None, :], 0.0), axis=2)
    return hidden_grad[None, None], gate_grad[None]


def column_parts(width):
    tiles = width // 128
    few = tiles * 3 // 28
    many = (tiles - 2 * few) // 2
    sizes = (many, tiles - 2 * few - many, few, few)
    parts, at = [], 0
    for order, size in zip(("zxy", "zyx", "xyz", "yxz"), sizes):
        if size:
            parts.append((order, at * 128, size * 128))
        at += size
    return parts


def relay_kernel(
    most, parts, grad_ref, meta_ref, down_hbm, saved_hbm, hidden_out, gate_out,
    tok, meta_all, down, saved, hidden, rows, back, sent_back, came_back,
    swap_sems, send_sems, recv_sems, meta_send, meta_recv, back_send, back_recv, local_sems,
):
    experts, tokens, width = tok.shape
    top = meta_ref.shape[0] // 2
    hidden_width = down.shape[0]
    section, me = lax.axis_index("section"), lax.axis_index("expert")
    other = 1 - section
    vz, vy, vx = me // 4, (me // 2) % 2, me % 2

    def at(z, y, x):
        return z * 4 + y * 2 + x

    x_peer, y_peer = at(vz, vy, 1 - vx), at(vz, 1 - vy, vx)

    load_down = pltpu.make_async_copy(down_hbm, down, local_sems.at[0])
    load_saved = pltpu.make_async_copy(saved_hbm, saved, local_sems.at[1])
    load_down.start()
    load_saved.start()

    barrier = pltpu.get_barrier_semaphore()

    def greet(sec, exp):
        pl.semaphore_signal(barrier, inc=1, device_id=(sec, exp), device_id_type=MESH)

    greet(other, me)
    greet(other, x_peer)
    greet(other, y_peer)
    pl.when(vz < DEPTH - 1)(lambda: greet(other, me + 4))
    pl.when(vz > 0)(lambda: greet(other, me - 4))

    @pl.loop(1, experts)
    def _(j):
        greet(section, (me + j) % experts)

    inner = (vz + 2) // 3 - vz // 3
    pl.semaphore_wait(barrier, experts + 3 + inner)

    half = vz // 2
    near = vz + half * (3 - 2 * vz)

    def block_of(k, dx, dy):
        z = (near, 1 - near, 2, 3)[k]
        z = z + half * (3 - 2 * z)
        return z, at(z, vy + dy * (1 - 2 * vy), vx + dx * (1 - 2 * vx))

    def hop(p, item, way, block, sec, peer, src):
        _, lo, size = parts[p]
        return pltpu.make_async_remote_copy(
            src_ref=src.at[:, pl.ds(lo, size)],
            dst_ref=tok.at[block, :, pl.ds(lo, size)],
            send_sem=send_sems.at[(p * experts + item) * 4 + way],
            recv_sem=recv_sems.at[p * experts + block],
            device_id=(sec, peer),
            device_id_type=MESH,
        )

    def hops(p, item, k, dx, dy, act):
        order = parts[p][0]
        z, block = block_of(k, dx, dy)
        own = k == 0 and dx == 0 and dy == 0
        src, sec = (grad_ref, other) if own else (tok.at[block], section)
        moved = {"x": dx, "y": dy, "z": k}
        for place, way in enumerate(order):
            if any(moved[d] for d in order[place + 1:]):
                continue
            if way == "x" and not dx:
                act(hop(p, item, 0, block, sec, x_peer, src))
            if way == "y" and not dy:
                act(hop(p, item, 1, block, sec, y_peer, src))
            if way == "z":
                pl.when(jnp.logical_and(vz < DEPTH - 1, z <= vz))(
                    lambda: act(hop(p, item, 2, block, sec, me + 4, src))
                )
                pl.when(jnp.logical_and(vz > 0, z >= vz))(
                    lambda: act(hop(p, item, 3, block, sec, me - 4, src))
                )

    items = sorted(
        ((k, dx, dy) for k in range(DEPTH) for dx in range(2) for dy in range(2)),
        key=lambda it: (sum(it), -it[0]),
    )

    def meta_copy(j):
        peer = (me + j) % experts
        return pltpu.make_async_remote_copy(
            src_ref=meta_ref, dst_ref=meta_all.at[me], send_sem=meta_send.at[j],
            recv_sem=meta_recv.at[me], device_id=(section, peer), device_id_type=MESH,
        )

    def meta_arrival(j):
        peer = (me + j) % experts
        return pltpu.make_async_remote_copy(
            src_ref=meta_ref, dst_ref=meta_all.at[peer], send_sem=meta_send.at[j],
            recv_sem=meta_recv.at[peer], device_id=(section, peer), device_id_type=MESH,
        )

    def swap_copy():
        return pltpu.make_async_remote_copy(
            src_ref=grad_ref, dst_ref=tok.at[me], send_sem=swap_sems.at[0],
            recv_sem=swap_sems.at[1], device_id=(other, me), device_id_type=MESH,
        )

    def back_copy(item, block):
        return pltpu.make_async_remote_copy(
            src_ref=sent_back.at[block], dst_ref=came_back.at[me], send_sem=back_send.at[item],
            recv_sem=back_recv.at[me], device_id=(section, block), device_id_type=MESH,
        )

    def back_arrival(item, block):
        return pltpu.make_async_remote_copy(
            src_ref=sent_back.at[block], dst_ref=came_back.at[block], send_sem=back_send.at[item],
            recv_sem=back_recv.at[block], device_id=(section, block), device_id_type=MESH,
        )

    start = lambda copy: copy.start()
    for p in range(len(parts)):
        hops(p, 0, 0, 0, 0, start)
    swap_copy().start()

    @pl.loop(1, experts)
    def _(j):
        meta_copy(j).start()

    meta_all[me] = meta_ref[...]

    def take(item):
        k, dx, dy = items[item]
        _, block = block_of(k, dx, dy)
        for p in range(len(parts)):
            hop(p, item, 0, block, section, x_peer, tok.at[block]).wait_recv()
            hops(p, item, k, dx, dy, start)

    iota = lambda shape, dim: lax.broadcasted_iota(jnp.int32, shape, dim).astype(jnp.float32)

    def owners(block):
        ids = meta_all[block, pl.ds(0, top), :]
        gates = meta_all[block, pl.ds(top, top), :]
        named = ids == me.astype(jnp.float32)
        owned = jnp.sum(jnp.where(named, 1.0, 0.0), axis=0, keepdims=True)
        gate = jnp.sum(jnp.where(named, gates, 0.0), axis=0, keepdims=True)
        earlier = jnp.where(iota((tokens, tokens), 0) < iota((tokens, tokens), 1), 1.0, 0.0)
        before = jnp.dot(
            jnp.broadcast_to(owned, (16, tokens)).astype(jnp.bfloat16),
            earlier.astype(jnp.bfloat16),
            preferred_element_type=jnp.float32,
        )[:1]
        rank = jnp.where(owned > 0.5, before, -1.0)
        return iota((most, tokens), 0) == rank, gate

    def work(first):
        blocks = [block_of(*items[first + i])[1] for i in range(BATCH)]
        for i, block in enumerate(blocks):
            select, _ = owners(block)
            rows[pl.ds(i * most, most), :] = jnp.dot(
                jnp.where(select, 1.0, 0.0).astype(jnp.bfloat16), tok[block],
                preferred_element_type=jnp.float32,
            ).astype(jnp.bfloat16)

        @pl.loop(0, hidden_width // 256)
        def _(j):
            at_j = pl.ds(pl.multiple_of(j * 256, 256), 256)
            back[:, at_j] = lax.dot_general(
                rows[...], down[at_j, :], (((1,), (1,)), ((), ())),
                preferred_element_type=jnp.float32,
            )

        for i, block in enumerate(blocks):
            select, gate = owners(block)
            weight = jnp.sum(jnp.where(select, gate, 0.0), axis=1, keepdims=True)
            value = back[pl.ds(i * most, most), :]
            hidden[block] = (weight * value).astype(jnp.bfloat16)
            slot = jnp.sum(saved[block].astype(jnp.float32) * value, axis=1, keepdims=True)
            by_token = jnp.sum(jnp.where(select, slot, 0.0), axis=0, keepdims=True)
            by_token = jnp.broadcast_to(by_token, (8, tokens))
            if first + i == 0:
                came_back[block] = by_token
            else:
                sent_back[block] = by_token
                back_copy(first + i, block).start()
            hidden_store(first + i, block).start()

    def hidden_store(item, block):
        return pltpu.make_async_copy(hidden.at[block], hidden_out.at[block], local_sems.at[2 + item])

    for item in range(1, 8):
        take(item)

    @pl.loop(1, experts)
    def _(j):
        meta_arrival(j).wait_recv()

    swap_copy().wait_recv()
    load_down.wait()
    load_saved.wait()
    work(0)
    for item in range(8, 12):
        take(item)
    work(4)
    for item in range(12, 15):
        take(item)
    work(8)
    take(15)
    work(12)

    for item, (k, dx, dy) in enumerate(items):
        block = block_of(k, dx, dy)[1]
        hidden_store(item, block).wait()
        for p in range(len(parts)):
            hops(p, item, k, dx, dy, lambda copy: copy.wait_send())
    swap_copy().wait_send()

    @pl.loop(1, experts)
    def _(j):
        meta_copy(j).wait_send()

    for item in range(1, experts):
        block = block_of(*items[item])[1]
        back_arrival(item, block).wait_recv()
        back_copy(item, block).wait_send()
    ids = meta_ref[pl.ds(0, top), :]
    total = jnp.zeros((top, tokens), jnp.float32)
    for e in range(experts):
        total += jnp.where(ids == float(e), came_back[e], 0.0)
    gate_out[...] = total


def relayed(grad_out, expert_ids, gate_weights, down_weight, hidden_saved):
    experts = lax.axis_size("expert")
    tokens, width = grad_out.shape[1:]
    most, hidden_width = hidden_saved.shape[3:]
    top = expert_ids.shape[2]
    meta = jnp.concatenate(
        [expert_ids[0].T.astype(jnp.float32), gate_weights[0].T.astype(jnp.float32)], axis=0
    )
    parts = column_parts(width)
    f32, bf16 = jnp.float32, jnp.bfloat16
    dma = pltpu.SemaphoreType.DMA
    vmem, any_space = pl.BlockSpec(memory_space=pltpu.VMEM), pl.BlockSpec(memory_space=pl.ANY)
    hidden_grad, gate_rows = pl.pallas_call(
        functools.partial(relay_kernel, most, parts),
        out_shape=(
            jax.ShapeDtypeStruct((experts, most, hidden_width), bf16),
            jax.ShapeDtypeStruct((top, tokens), f32),
        ),
        in_specs=[vmem, vmem, any_space, any_space],
        out_specs=(any_space, vmem),
        scratch_shapes=[
            pltpu.VMEM((experts, tokens, width), bf16),
            pltpu.VMEM((experts, 2 * top, tokens), f32),
            pltpu.VMEM((hidden_width, width), bf16),
            pltpu.VMEM((experts, most, hidden_width), bf16),
            pltpu.VMEM((experts, most, hidden_width), bf16),
            pltpu.VMEM((BATCH * most, width), bf16),
            pltpu.VMEM((BATCH * most, hidden_width), f32),
            pltpu.VMEM((experts, 8, tokens), f32),
            pltpu.VMEM((experts, 8, tokens), f32),
            dma((2,)),
            dma((len(parts) * experts * 4,)),
            dma((len(parts) * experts,)),
            dma((experts,)),
            dma((experts,)),
            dma((experts,)),
            dma((experts,)),
            dma((2 + experts,)),
        ],
        compiler_params=pltpu.CompilerParams(
            collective_id=0, has_side_effects=True, vmem_limit_bytes=56 * 1024 * 1024
        ),
        cost_estimate=pl.CostEstimate(
            flops=2 * experts * most * width * hidden_width, bytes_accessed=16 * 1024 * 1024, transcendentals=0
        ),
    )(grad_out[0], meta, down_weight[0, 0], hidden_saved[0, 0])
    return hidden_grad[None, None], gate_rows.T[None]


def fits_relay(mesh):
    return mesh.shape["section"] == 2 and mesh.shape["expert"] == DEPTH * 4


def solution(mesh):
    in_specs = (
        P("section", "expert", None),
        P("section", "expert", None),
        P("section", "expert", None),
        P("section", "expert", None, None),
        P("section", "expert", None, None, None),
    )
    out_specs = (P("section", "expert", None, None, None), P("section", "expert", None))
    local_step = relayed if fits_relay(mesh) else gathered
    return jax.shard_map(local_step, mesh=mesh, in_specs=in_specs, out_specs=out_specs, check_vma=False)
```

```python
import functools

import jax
import jax.numpy as jnp
from jax import lax
from jax.experimental import pallas as pl
from jax.experimental.pallas import tpu as pltpu
from jax.sharding import PartitionSpec as P

MESH = pl.DeviceIdType.MESH
DEPTH, BATCH = 4, 4


def shifted(x, axis, by):
    size = lax.axis_size(axis)
    return lax.ppermute(x, axis, [(i, (i + by) % size) for i in range(size)])


def project_back(rows_in, weight_part):
    flat_rows = rows_in.reshape(-1, rows_in.shape[2])
    return lax.dot_general(
        flat_rows, weight_part, (((1,), (1,)), ((), ())), preferred_element_type=jnp.float32
    )


def gathered(grad_out, expert_ids, gate_weights, down_weight, hidden_saved):
    experts = lax.axis_size("expert")
    most = hidden_saved.shape[3]
    width = grad_out.shape[2]
    tokens = grad_out.shape[1]
    hidden_width = down_weight.shape[2]
    me = lax.axis_index("expert")
    ids = lax.all_gather(expert_ids[0], "expert", axis=0)
    gates = lax.all_gather(gate_weights[0], "expert", axis=0)
    incoming = shifted(grad_out[0], "section", -1)
    grads = lax.all_gather(incoming, "expert", axis=0)
    named = ids == me
    owned = jnp.any(named, axis=2)
    place = jnp.arange(tokens, dtype=jnp.int32)
    earlier = (place[:, None] < place[None, :]).astype(jnp.bfloat16)
    before = jnp.dot(owned.astype(jnp.bfloat16), earlier, preferred_element_type=jnp.float32)
    rank = jnp.where(owned, before.astype(jnp.int32), -1)
    gate = jnp.sum(jnp.where(named, gates.astype(jnp.float32), 0.0), axis=2)
    select = rank[:, None, :] == jnp.arange(most, dtype=jnp.int32)[None, :, None]
    rows = lax.dot_general(
        select.astype(jnp.bfloat16), grads, (((2,), (1,)), ((0,), (0,))), preferred_element_type=jnp.bfloat16
    )
    back = project_back(rows, down_weight[0, 0]).reshape(experts, most, hidden_width)
    weight = jnp.sum(jnp.where(select, gate[:, None, :], 0.0), axis=2)
    hidden_grad = (weight[:, :, None] * back).astype(jnp.bfloat16)
    slot_grad = jnp.sum(hidden_saved[0, 0].astype(jnp.float32) * back, axis=2)
    by_token = jnp.sum(jnp.where(select, slot_grad[:, :, None], 0.0), axis=1)
    returned = lax.all_to_all(by_token, "expert", split_axis=0, concat_axis=0, tiled=True)
    mine = expert_ids[0][:, :, None] == jnp.arange(experts, dtype=jnp.int32)
    gate_grad = jnp.sum(jnp.where(mine, returned.T[:, None, :], 0.0), axis=2)
    return hidden_grad[None, None], gate_grad[None]


def column_parts(width):
    tiles = width // 128
    few = tiles * 1 // 28
    many = (tiles - 2 * few) // 2
    sizes = (many, tiles - 2 * few - many, few, few)
    parts, at = [], 0
    for order, size in zip(("zxy", "zyx", "xyz", "yxz"), sizes):
        if size:
            parts.append((order, at * 128, size * 128))
        at += size
    return parts


def relay_kernel(
    most, parts, grad_ref, ids_ref, gates_ref, down_hbm, saved_hbm, hidden_out, gate_out,
    tok, meta_ref, meta_all, meta_other, ranks, down, saved, hidden, rows, packed, back, sent_back, came_back,
    swap_sems, send_sems, recv_sems, meta_send, meta_recv, back_send, back_recv, local_sems,
):
    experts, tokens, width = tok.shape
    top = meta_ref.shape[0] // 2
    hidden_width = down.shape[0]
    section, me = lax.axis_index("section"), lax.axis_index("expert")
    other = 1 - section
    vz, vy, vx = me // 4, (me // 2) % 2, me % 2

    def at(z, y, x):
        return z * 4 + y * 2 + x

    x_peer, y_peer = at(vz, vy, 1 - vx), at(vz, 1 - vy, vx)
    iota = lambda shape, dim: lax.broadcasted_iota(jnp.int32, shape, dim).astype(jnp.float32)

    load_down = pltpu.make_async_copy(down_hbm, down, local_sems.at[0])
    load_saved = pltpu.make_async_copy(saved_hbm, saved, local_sems.at[1])
    load_down.start()
    load_saved.start()

    barrier = pltpu.get_barrier_semaphore()

    def greet(sec, exp):
        pl.semaphore_signal(barrier, inc=1, device_id=(sec, exp), device_id_type=MESH)

    greet(other, me)
    greet(other, x_peer)
    greet(other, y_peer)
    pl.when(vz < DEPTH - 1)(lambda: greet(other, me + 4))
    pl.when(vz > 0)(lambda: greet(other, me - 4))

    @pl.loop(1, experts)
    def _(j):
        greet(section, (me + j) % experts)

    inner = (vz + 2) // 3 - vz // 3
    pl.semaphore_wait(barrier, experts + 3 + inner)

    half = vz // 2
    near = vz + half * (3 - 2 * vz)

    def block_of(k, dx, dy):
        z = (near, 1 - near, 2, 3)[k]
        z = z + half * (3 - 2 * z)
        return z, at(z, vy + dy * (1 - 2 * vy), vx + dx * (1 - 2 * vx))

    def hop(p, item, way, block, sec, peer, src):
        _, lo, size = parts[p]
        return pltpu.make_async_remote_copy(
            src_ref=src.at[:, pl.ds(lo, size)],
            dst_ref=tok.at[block, :, pl.ds(lo, size)],
            send_sem=send_sems.at[(p * experts + item) * 4 + way],
            recv_sem=recv_sems.at[p * experts + block],
            device_id=(sec, peer),
            device_id_type=MESH,
        )

    items = sorted(
        ((k, dx, dy) for k in range(DEPTH) for dx in range(2) for dy in range(2)),
        key=lambda it: (sum(it), -it[0]),
    )

    def is_packed(p, item):
        return parts[p][0][0] == "z" and bool(items[item]["zxy".index(parts[p][0][2])])

    def packed_hop(p, item, way):
        order, lo, size = parts[p]
        k, dx, dy = items[item]
        block = block_of(k, dx, dy)[1]
        there = items.index((k, 1, dy) if way == 0 else (k, dx, 1))
        slot = [it for it in items if not it["zxy".index(order[2])]].index((k, dx, dy))
        return slot, pltpu.make_async_remote_copy(
            src_ref=packed.at[p, slot, :, pl.ds(0, size)],
            dst_ref=rows.at[there, :, pl.ds(lo, size)],
            send_sem=send_sems.at[(p * experts + item) * 4 + way],
            recv_sem=recv_sems.at[p * experts + block],
            device_id=(other if item == 0 else section, x_peer if way == 0 else y_peer),
            device_id_type=MESH,
        )

    def packed_way(p, item):
        order = parts[p][0]
        if order[0] != "z" or is_packed(p, item):
            return None
        return "xy".index(order[2])

    def pack_and_send(p, item, rank):
        way = packed_way(p, item)
        slot, copy = packed_hop(p, item, way)
        _, lo, size = parts[p]
        block = block_of(*items[item])[1]
        source = grad_ref[:, pl.ds(lo, size)] if item == 0 else tok[block, :, pl.ds(lo, size)]
        packed[p, slot, :, pl.ds(0, size)] = chosen(rank, source)
        copy.start()

    def chosen(rank, source):
        select = iota((most, tokens), 0) == rank
        return jnp.dot(
            jnp.where(select, 1.0, 0.0).astype(jnp.bfloat16), source, preferred_element_type=jnp.float32
        ).astype(jnp.bfloat16)

    def hops(p, item, k, dx, dy, act):
        order = parts[p][0]
        z, block = block_of(k, dx, dy)
        own = k == 0 and dx == 0 and dy == 0
        src, sec = (grad_ref, other) if own else (tok.at[block], section)
        moved = {"x": dx, "y": dy, "z": k}
        for place, way in enumerate(order):
            if any(moved[d] for d in order[place + 1:]):
                continue
            if order[0] == "z" and place == 2:
                continue
            if way == "x" and not dx:
                act(hop(p, item, 0, block, sec, x_peer, src))
            if way == "y" and not dy:
                act(hop(p, item, 1, block, sec, y_peer, src))
            if way == "z":
                pl.when(jnp.logical_and(vz < DEPTH - 1, z <= vz))(
                    lambda: act(hop(p, item, 2, block, sec, me + 4, src))
                )
                pl.when(jnp.logical_and(vz > 0, z >= vz))(
                    lambda: act(hop(p, item, 3, block, sec, me - 4, src))
                )

    def meta_copy(j):
        peer = (me + j) % experts
        return pltpu.make_async_remote_copy(
            src_ref=meta_ref, dst_ref=meta_all.at[me], send_sem=meta_send.at[j],
            recv_sem=meta_recv.at[me], device_id=(section, peer), device_id_type=MESH,
        )

    def meta_arrival(j):
        peer = (me + j) % experts
        return pltpu.make_async_remote_copy(
            src_ref=meta_ref, dst_ref=meta_all.at[peer], send_sem=meta_send.at[j],
            recv_sem=meta_recv.at[peer], device_id=(section, peer), device_id_type=MESH,
        )

    def swap_copy():
        return pltpu.make_async_remote_copy(
            src_ref=grad_ref, dst_ref=tok.at[me], send_sem=swap_sems.at[0],
            recv_sem=swap_sems.at[1], device_id=(other, me), device_id_type=MESH,
        )

    def meta_swap():
        return pltpu.make_async_remote_copy(
            src_ref=meta_ref, dst_ref=meta_other, send_sem=swap_sems.at[2],
            recv_sem=swap_sems.at[3], device_id=(other, me), device_id_type=MESH,
        )

    def back_copy(item, block):
        return pltpu.make_async_remote_copy(
            src_ref=sent_back.at[block], dst_ref=came_back.at[me], send_sem=back_send.at[item],
            recv_sem=back_recv.at[me], device_id=(section, block), device_id_type=MESH,
        )

    def back_arrival(item, block):
        return pltpu.make_async_remote_copy(
            src_ref=sent_back.at[block], dst_ref=came_back.at[block], send_sem=back_send.at[item],
            recv_sem=back_recv.at[block], device_id=(section, block), device_id_type=MESH,
        )

    start = lambda copy: copy.start()
    for p in range(len(parts)):
        hops(p, 0, 0, 0, 0, start)
    meta_ref[pl.ds(0, top), :] = ids_ref[...].astype(jnp.float32)
    meta_ref[pl.ds(top, top), :] = gates_ref[...].astype(jnp.float32)
    meta_swap().start()

    @pl.loop(1, experts)
    def _(j):
        meta_copy(j).start()

    meta_all[me] = meta_ref[...]
    swap_copy().start()

    def owned_by(ids, expert):
        return jnp.max(jnp.where(ids == expert.astype(jnp.float32), 1.0, 0.0), axis=0, keepdims=True)

    def ranks_of(owned):
        earlier = jnp.where(iota((tokens, tokens), 0) < iota((tokens, tokens), 1), 1.0, 0.0)
        before = jnp.dot(
            owned.astype(jnp.bfloat16), earlier.astype(jnp.bfloat16), preferred_element_type=jnp.float32
        )
        return jnp.where(owned > 0.5, before, -1.0)

    meta_swap().wait_recv()
    ids = meta_other[pl.ds(0, top), :]
    owned = [owned_by(ids, peer) for peer in (x_peer, y_peer)]
    own_ranks = ranks_of(jnp.concatenate([owned[0]] * 8 + [owned[1]] * 8, axis=0))
    for p in range(len(parts)):
        way = packed_way(p, 0)
        if way is not None:
            pack_and_send(p, 0, own_ranks[8 * way:8 * way + 1])

    @pl.loop(1, experts)
    def _(j):
        meta_arrival(j).wait_recv()

    for i, expert in enumerate((x_peer, y_peer, me)):
        table = jnp.concatenate(
            [owned_by(meta_all[b, pl.ds(0, top), :], expert) for b in range(experts)], axis=0
        )
        table = ranks_of(table)
        for b in range(experts):
            ranks[i, b] = table[b:b + 1]

    def take(item):
        k, dx, dy = items[item]
        _, block = block_of(k, dx, dy)
        for p in range(len(parts)):
            if is_packed(p, item):
                continue
            hop(p, item, 0, block, section, x_peer, tok.at[block]).wait_recv()
            hops(p, item, k, dx, dy, start)
            way = packed_way(p, item)
            if way is not None:
                pack_and_send(p, item, ranks[way, block])

    def finish(item):
        block = block_of(*items[item])[1]
        rank = ranks[2, block]
        for p, (_, lo, size) in enumerate(parts):
            if is_packed(p, item):
                pltpu.make_async_remote_copy(
                    src_ref=rows.at[item, :, pl.ds(lo, size)],
                    dst_ref=rows.at[item, :, pl.ds(lo, size)],
                    send_sem=send_sems.at[0],
                    recv_sem=recv_sems.at[p * experts + block],
                    device_id=(section, x_peer),
                    device_id_type=MESH,
                ).wait_recv()
            else:
                rows[item, :, pl.ds(lo, size)] = chosen(rank, tok[block, :, pl.ds(lo, size)])

    def work(first):
        blocks = [block_of(*items[first + i])[1] for i in range(BATCH)]
        for i in range(BATCH):
            finish(first + i)

        @pl.loop(0, hidden_width // 256)
        def _(j):
            at_j = pl.ds(pl.multiple_of(j * 256, 256), 256)
            back[:, at_j] = lax.dot_general(
                rows[pl.ds(first, BATCH)].reshape(BATCH * most, width), down[at_j, :], (((1,), (1,)), ((), ())),
                preferred_element_type=jnp.float32,
            )

        for i, block in enumerate(blocks):
            named = meta_all[block, pl.ds(0, top), :] == me.astype(jnp.float32)
            gate = jnp.where(named, meta_all[block, pl.ds(top, top), :], 0.0)
            gate = jnp.sum(gate, axis=0, keepdims=True)
            select = iota((most, tokens), 0) == ranks[2, block]
            weight = jnp.sum(jnp.where(select, gate, 0.0), axis=1, keepdims=True)
            value = back[pl.ds(i * most, most), :]
            hidden[block] = (weight * value).astype(jnp.bfloat16)
            slot = jnp.sum(saved[block].astype(jnp.float32) * value, axis=1, keepdims=True)
            by_token = jnp.sum(jnp.where(select, slot, 0.0), axis=0, keepdims=True)
            by_token = jnp.broadcast_to(by_token, (8, tokens))
            if first + i == 0:
                came_back[block] = by_token
            else:
                sent_back[block] = by_token
                back_copy(first + i, block).start()
            hidden_store(first + i, block).start()

    def hidden_store(item, block):
        return pltpu.make_async_copy(hidden.at[block], hidden_out.at[block], local_sems.at[2 + item])

    for item in range(1, 8):
        take(item)

    swap_copy().wait_recv()
    load_down.wait()
    load_saved.wait()
    work(0)
    for item in range(8, 12):
        take(item)
    work(4)
    for item in range(12, 15):
        take(item)
    work(8)
    take(15)
    work(12)

    for item, (k, dx, dy) in enumerate(items):
        block = block_of(k, dx, dy)[1]
        hidden_store(item, block).wait()
        for p in range(len(parts)):
            hops(p, item, k, dx, dy, lambda copy: copy.wait_send())
            way = packed_way(p, item)
            if way is not None:
                packed_hop(p, item, way)[1].wait_send()
    swap_copy().wait_send()
    meta_swap().wait_send()

    @pl.loop(1, experts)
    def _(j):
        meta_copy(j).wait_send()

    for item in range(1, experts):
        block = block_of(*items[item])[1]
        back_arrival(item, block).wait_recv()
        back_copy(item, block).wait_send()
    ids = meta_ref[pl.ds(0, top), :]
    total = jnp.zeros((top, tokens), jnp.float32)
    for e in range(experts):
        total += jnp.where(ids == float(e), came_back[e], 0.0)
    gate_out[...] = total


def relayed(grad_out, expert_ids, gate_weights, down_weight, hidden_saved):
    experts = lax.axis_size("expert")
    tokens, width = grad_out.shape[1:]
    most, hidden_width = hidden_saved.shape[3:]
    top = expert_ids.shape[2]
    parts = column_parts(width)
    f32, bf16 = jnp.float32, jnp.bfloat16
    dma = pltpu.SemaphoreType.DMA
    vmem, any_space = pl.BlockSpec(memory_space=pltpu.VMEM), pl.BlockSpec(memory_space=pl.ANY)
    hidden_grad, gate_rows = pl.pallas_call(
        functools.partial(relay_kernel, most, parts),
        out_shape=(
            jax.ShapeDtypeStruct((experts, most, hidden_width), bf16),
            jax.ShapeDtypeStruct((top, tokens), f32),
        ),
        in_specs=[vmem, vmem, vmem, any_space, any_space],
        out_specs=(any_space, vmem),
        scratch_shapes=[
            pltpu.VMEM((experts, tokens, width), bf16),
            pltpu.VMEM((2 * top, tokens), f32),
            pltpu.VMEM((experts, 2 * top, tokens), f32),
            pltpu.VMEM((2 * top, tokens), f32),
            pltpu.VMEM((3, experts, 1, tokens), f32),
            pltpu.VMEM((hidden_width, width), bf16),
            pltpu.VMEM((experts, most, hidden_width), bf16),
            pltpu.VMEM((experts, most, hidden_width), bf16),
            pltpu.VMEM((experts, most, width), bf16),
            pltpu.VMEM((2, 8, most, max(size for _, _, size in parts)), bf16),
            pltpu.VMEM((BATCH * most, hidden_width), f32),
            pltpu.VMEM((experts, 8, tokens), f32),
            pltpu.VMEM((experts, 8, tokens), f32),
            dma((4,)),
            dma((len(parts) * experts * 4,)),
            dma((len(parts) * experts,)),
            dma((experts,)),
            dma((experts,)),
            dma((experts,)),
            dma((experts,)),
            dma((2 + experts,)),
        ],
        compiler_params=pltpu.CompilerParams(
            collective_id=0, has_side_effects=True, vmem_limit_bytes=56 * 1024 * 1024
        ),
        cost_estimate=pl.CostEstimate(
            flops=2 * experts * most * width * hidden_width, bytes_accessed=16 * 1024 * 1024, transcendentals=0
        ),
    )(grad_out[0], expert_ids[0].T, gate_weights[0].T, down_weight[0, 0], hidden_saved[0, 0])
    return hidden_grad[None, None], gate_rows.T[None]


def fits_relay(mesh):
    return mesh.shape["section"] == 2 and mesh.shape["expert"] == DEPTH * 4


def solution(mesh):
    in_specs = (
        P("section", "expert", None),
        P("section", "expert", None),
        P("section", "expert", None),
        P("section", "expert", None, None),
        P("section", "expert", None, None, None),
    )
    out_specs = (P("section", "expert", None, None, None), P("section", "expert", None))
    local_step = relayed if fits_relay(mesh) else gathered
    return jax.shard_map(local_step, mesh=mesh, in_specs=in_specs, out_specs=out_specs, check_vma=False)
```

```python
import functools

import jax
import jax.numpy as jnp
from jax import lax
from jax.experimental import pallas as pl
from jax.experimental.pallas import tpu as pltpu
from jax.sharding import PartitionSpec as P

MESH = pl.DeviceIdType.MESH
DEPTH, BATCH = 4, 4


def shifted(x, axis, by):
    size = lax.axis_size(axis)
    return lax.ppermute(x, axis, [(i, (i + by) % size) for i in range(size)])


def project_back(rows_in, weight_part):
    flat_rows = rows_in.reshape(-1, rows_in.shape[2])
    return lax.dot_general(
        flat_rows, weight_part, (((1,), (1,)), ((), ())), preferred_element_type=jnp.float32
    )


def gathered(grad_out, expert_ids, gate_weights, down_weight, hidden_saved):
    experts = lax.axis_size("expert")
    most = hidden_saved.shape[3]
    width = grad_out.shape[2]
    tokens = grad_out.shape[1]
    hidden_width = down_weight.shape[2]
    me = lax.axis_index("expert")
    ids = lax.all_gather(expert_ids[0], "expert", axis=0)
    gates = lax.all_gather(gate_weights[0], "expert", axis=0)
    incoming = shifted(grad_out[0], "section", -1)
    grads = lax.all_gather(incoming, "expert", axis=0)
    named = ids == me
    owned = jnp.any(named, axis=2)
    place = jnp.arange(tokens, dtype=jnp.int32)
    earlier = (place[:, None] < place[None, :]).astype(jnp.bfloat16)
    before = jnp.dot(owned.astype(jnp.bfloat16), earlier, preferred_element_type=jnp.float32)
    rank = jnp.where(owned, before.astype(jnp.int32), -1)
    gate = jnp.sum(jnp.where(named, gates.astype(jnp.float32), 0.0), axis=2)
    select = rank[:, None, :] == jnp.arange(most, dtype=jnp.int32)[None, :, None]
    rows = lax.dot_general(
        select.astype(jnp.bfloat16), grads, (((2,), (1,)), ((0,), (0,))), preferred_element_type=jnp.bfloat16
    )
    back = project_back(rows, down_weight[0, 0]).reshape(experts, most, hidden_width)
    weight = jnp.sum(jnp.where(select, gate[:, None, :], 0.0), axis=2)
    hidden_grad = (weight[:, :, None] * back).astype(jnp.bfloat16)
    slot_grad = jnp.sum(hidden_saved[0, 0].astype(jnp.float32) * back, axis=2)
    by_token = jnp.sum(jnp.where(select, slot_grad[:, :, None], 0.0), axis=1)
    returned = lax.all_to_all(by_token, "expert", split_axis=0, concat_axis=0, tiled=True)
    mine = expert_ids[0][:, :, None] == jnp.arange(experts, dtype=jnp.int32)
    gate_grad = jnp.sum(jnp.where(mine, returned.T[:, None, :], 0.0), axis=2)
    return hidden_grad[None, None], gate_grad[None]


def column_parts(width):
    tiles = width // 128
    few = tiles * 1 // 28
    many = (tiles - 2 * few) // 2
    sizes = (many, tiles - 2 * few - many, few, few)
    parts, at = [], 0
    for order, size in zip(("zxy", "zyx", "xyz", "yxz"), sizes):
        if size:
            parts.append((order, at * 128, size * 128))
        at += size
    return parts


def relay_kernel(
    most, parts, grad_ref, ids_ref, gates_ref, down_hbm, saved_hbm, hidden_out, gate_out,
    tok, meta_ref, meta_all, meta_other, ranks, down, saved, hidden, rows, packed, back, sent_back, came_back,
    swap_sems, send_sems, recv_sems, meta_send, meta_recv, back_send, back_recv, local_sems,
):
    experts, tokens, width = tok.shape
    top = meta_ref.shape[0] // 2
    hidden_width = down.shape[0]
    section, me = lax.axis_index("section"), lax.axis_index("expert")
    other = 1 - section
    vz, vy, vx = me // 4, (me // 2) % 2, me % 2

    def at(z, y, x):
        return z * 4 + y * 2 + x

    x_peer, y_peer = at(vz, vy, 1 - vx), at(vz, 1 - vy, vx)
    iota = lambda shape, dim: lax.broadcasted_iota(jnp.int32, shape, dim).astype(jnp.float32)

    load_down = pltpu.make_async_copy(down_hbm, down, local_sems.at[0])
    load_saved = pltpu.make_async_copy(saved_hbm, saved, local_sems.at[1])
    load_down.start()
    load_saved.start()

    barrier = pltpu.get_barrier_semaphore()

    def greet(sec, exp):
        pl.semaphore_signal(barrier, inc=1, device_id=(sec, exp), device_id_type=MESH)

    greet(other, me)
    greet(other, x_peer)
    greet(other, y_peer)
    pl.when(vz < DEPTH - 1)(lambda: greet(other, me + 4))
    pl.when(vz > 0)(lambda: greet(other, me - 4))

    @pl.loop(1, experts)
    def _(j):
        greet(section, (me + j) % experts)

    inner = (vz + 2) // 3 - vz // 3
    pl.semaphore_wait(barrier, experts + 3 + inner)

    half = vz // 2
    near = vz + half * (3 - 2 * vz)

    def block_of(k, dx, dy):
        z = (near, 1 - near, 2, 3)[k]
        z = z + half * (3 - 2 * z)
        return z, at(z, vy + dy * (1 - 2 * vy), vx + dx * (1 - 2 * vx))

    def hop(p, item, way, block, sec, peer, src):
        _, lo, size = parts[p]
        return pltpu.make_async_remote_copy(
            src_ref=src.at[:, pl.ds(lo, size)],
            dst_ref=tok.at[block, :, pl.ds(lo, size)],
            send_sem=send_sems.at[(p * experts + item) * 4 + way],
            recv_sem=recv_sems.at[p * experts + block],
            device_id=(sec, peer),
            device_id_type=MESH,
        )

    items = sorted(
        ((k, dx, dy) for k in range(DEPTH) for dx in range(2) for dy in range(2)),
        key=lambda it: (sum(it), -it[0]),
    )

    def is_packed(p, item):
        return parts[p][0][0] == "z" and bool(items[item]["zxy".index(parts[p][0][2])])

    def packed_hop(p, item, way):
        order, lo, size = parts[p]
        k, dx, dy = items[item]
        block = block_of(k, dx, dy)[1]
        there = items.index((k, 1, dy) if way == 0 else (k, dx, 1))
        slot = [it for it in items if not it["zxy".index(order[2])]].index((k, dx, dy))
        return slot, pltpu.make_async_remote_copy(
            src_ref=packed.at[p, slot, :, pl.ds(0, size)],
            dst_ref=rows.at[there, :, pl.ds(lo, size)],
            send_sem=send_sems.at[(p * experts + item) * 4 + way],
            recv_sem=recv_sems.at[p * experts + block],
            device_id=(other if item == 0 else section, x_peer if way == 0 else y_peer),
            device_id_type=MESH,
        )

    def packed_way(p, item):
        order = parts[p][0]
        if order[0] != "z" or is_packed(p, item):
            return None
        return "xy".index(order[2])

    def pack_and_send(p, item, rank):
        way = packed_way(p, item)
        slot, copy = packed_hop(p, item, way)
        _, lo, size = parts[p]
        block = block_of(*items[item])[1]
        source = grad_ref[:, pl.ds(lo, size)] if item == 0 else tok[block, :, pl.ds(lo, size)]
        packed[p, slot, :, pl.ds(0, size)] = chosen(rank, source)
        copy.start()

    def chosen(rank, source):
        select = iota((most, tokens), 0) == rank
        return jnp.dot(
            jnp.where(select, 1.0, 0.0).astype(jnp.bfloat16), source, preferred_element_type=jnp.float32
        ).astype(jnp.bfloat16)

    def hops(p, item, k, dx, dy, act):
        order = parts[p][0]
        z, block = block_of(k, dx, dy)
        own = k == 0 and dx == 0 and dy == 0
        src, sec = (grad_ref, other) if own else (tok.at[block], section)
        moved = {"x": dx, "y": dy, "z": k}
        for place, way in enumerate(order):
            if any(moved[d] for d in order[place + 1:]):
                continue
            if order[0] == "z" and place == 2:
                continue
            if way == "x" and not dx:
                act(hop(p, item, 0, block, sec, x_peer, src))
            if way == "y" and not dy:
                act(hop(p, item, 1, block, sec, y_peer, src))
            if way == "z":
                pl.when(jnp.logical_and(vz < DEPTH - 1, z <= vz))(
                    lambda: act(hop(p, item, 2, block, sec, me + 4, src))
                )
                pl.when(jnp.logical_and(vz > 0, z >= vz))(
                    lambda: act(hop(p, item, 3, block, sec, me - 4, src))
                )

    def meta_copy(j):
        peer = (me + j) % experts
        return pltpu.make_async_remote_copy(
            src_ref=meta_ref, dst_ref=meta_all.at[me], send_sem=meta_send.at[j],
            recv_sem=meta_recv.at[me], device_id=(section, peer), device_id_type=MESH,
        )

    def meta_arrival(j):
        peer = (me + j) % experts
        return pltpu.make_async_remote_copy(
            src_ref=meta_ref, dst_ref=meta_all.at[peer], send_sem=meta_send.at[j],
            recv_sem=meta_recv.at[peer], device_id=(section, peer), device_id_type=MESH,
        )

    def swap_copy():
        return pltpu.make_async_remote_copy(
            src_ref=grad_ref, dst_ref=tok.at[me], send_sem=swap_sems.at[0],
            recv_sem=swap_sems.at[1], device_id=(other, me), device_id_type=MESH,
        )

    def meta_swap():
        return pltpu.make_async_remote_copy(
            src_ref=meta_ref, dst_ref=meta_other, send_sem=swap_sems.at[2],
            recv_sem=swap_sems.at[3], device_id=(other, me), device_id_type=MESH,
        )

    def back_copy(item, block):
        return pltpu.make_async_remote_copy(
            src_ref=sent_back.at[block], dst_ref=came_back.at[me], send_sem=back_send.at[item],
            recv_sem=back_recv.at[me], device_id=(section, block), device_id_type=MESH,
        )

    def back_arrival(item, block):
        return pltpu.make_async_remote_copy(
            src_ref=sent_back.at[block], dst_ref=came_back.at[block], send_sem=back_send.at[item],
            recv_sem=back_recv.at[block], device_id=(section, block), device_id_type=MESH,
        )

    start = lambda copy: copy.start()
    for p in range(len(parts)):
        hops(p, 0, 0, 0, 0, start)
    meta_ref[pl.ds(0, top), :] = ids_ref[...].astype(jnp.float32)
    meta_ref[pl.ds(top, top), :] = gates_ref[...].astype(jnp.float32)
    meta_swap().start()

    @pl.loop(1, experts)
    def _(j):
        meta_copy(j).start()

    meta_all[me] = meta_ref[...]
    swap_copy().start()

    def owned_by(ids, expert):
        return jnp.max(jnp.where(ids == expert.astype(jnp.float32), 1.0, 0.0), axis=0, keepdims=True)

    def ranks_of(owned):
        earlier = jnp.where(iota((tokens, tokens), 0) < iota((tokens, tokens), 1), 1.0, 0.0)
        before = jnp.dot(
            owned.astype(jnp.bfloat16), earlier.astype(jnp.bfloat16), preferred_element_type=jnp.float32
        )
        return jnp.where(owned > 0.5, before, -1.0)

    meta_swap().wait_recv()
    ids = meta_other[pl.ds(0, top), :]
    owned = [owned_by(ids, peer) for peer in (x_peer, y_peer)]
    own_ranks = ranks_of(jnp.concatenate([owned[0]] * 8 + [owned[1]] * 8, axis=0))
    for p in range(len(parts)):
        way = packed_way(p, 0)
        if way is not None:
            pack_and_send(p, 0, own_ranks[8 * way:8 * way + 1])

    @pl.loop(1, experts)
    def _(j):
        meta_arrival(j).wait_recv()

    for i, expert in enumerate((x_peer, y_peer, me)):
        table = jnp.concatenate(
            [owned_by(meta_all[b, pl.ds(0, top), :], expert) for b in range(experts)], axis=0
        )
        table = ranks_of(table)
        for b in range(experts):
            ranks[i, b] = table[b:b + 1]

    def take(item):
        k, dx, dy = items[item]
        _, block = block_of(k, dx, dy)
        for p in range(len(parts)):
            if is_packed(p, item):
                continue
            hop(p, item, 0, block, section, x_peer, tok.at[block]).wait_recv()
            hops(p, item, k, dx, dy, start)
            way = packed_way(p, item)
            if way is not None:
                pack_and_send(p, item, ranks[way, block])

    def finish(item):
        block = block_of(*items[item])[1]
        rank = ranks[2, block]
        for p, (_, lo, size) in enumerate(parts):
            if is_packed(p, item):
                pltpu.make_async_remote_copy(
                    src_ref=rows.at[item, :, pl.ds(lo, size)],
                    dst_ref=rows.at[item, :, pl.ds(lo, size)],
                    send_sem=send_sems.at[0],
                    recv_sem=recv_sems.at[p * experts + block],
                    device_id=(section, x_peer),
                    device_id_type=MESH,
                ).wait_recv()
            else:
                rows[item, :, pl.ds(lo, size)] = chosen(rank, tok[block, :, pl.ds(lo, size)])

    def work(first):
        blocks = [block_of(*items[first + i])[1] for i in range(BATCH)]
        for i in range(BATCH):
            finish(first + i)

        @pl.loop(0, hidden_width // 512)
        def _(j):
            at_j = pl.ds(pl.multiple_of(j * 512, 512), 512)
            back[:, at_j] = lax.dot_general(
                rows[pl.ds(first, BATCH)].reshape(BATCH * most, width), down[at_j, :], (((1,), (1,)), ((), ())),
                preferred_element_type=jnp.float32,
            )

        for i, block in enumerate(blocks):
            named = meta_all[block, pl.ds(0, top), :] == me.astype(jnp.float32)
            gate = jnp.where(named, meta_all[block, pl.ds(top, top), :], 0.0)
            gate = jnp.sum(gate, axis=0, keepdims=True)
            select = iota((most, tokens), 0) == ranks[2, block]
            weight = jnp.sum(jnp.where(select, gate, 0.0), axis=1, keepdims=True)
            value = back[pl.ds(i * most, most), :]
            hidden[block] = (weight * value).astype(jnp.bfloat16)
            slot = jnp.sum(saved[block].astype(jnp.float32) * value, axis=1, keepdims=True)
            by_token = jnp.sum(jnp.where(select, slot, 0.0), axis=0, keepdims=True)
            by_token = jnp.broadcast_to(by_token, (8, tokens))
            if first + i == 0:
                came_back[block] = by_token
            else:
                sent_back[block] = by_token
                back_copy(first + i, block).start()
            hidden_store(first + i, block).start()

    def hidden_store(item, block):
        return pltpu.make_async_copy(hidden.at[block], hidden_out.at[block], local_sems.at[2 + item])

    for item in range(1, 8):
        take(item)

    swap_copy().wait_recv()
    load_down.wait()
    load_saved.wait()
    work(0)
    for item in range(8, 12):
        take(item)
    work(4)
    for item in range(12, 15):
        take(item)
    work(8)
    take(15)
    work(12)

    for item, (k, dx, dy) in enumerate(items):
        block = block_of(k, dx, dy)[1]
        hidden_store(item, block).wait()
        for p in range(len(parts)):
            hops(p, item, k, dx, dy, lambda copy: copy.wait_send())
            way = packed_way(p, item)
            if way is not None:
                packed_hop(p, item, way)[1].wait_send()
    swap_copy().wait_send()
    meta_swap().wait_send()

    @pl.loop(1, experts)
    def _(j):
        meta_copy(j).wait_send()

    for item in range(1, experts):
        block = block_of(*items[item])[1]
        back_arrival(item, block).wait_recv()
        back_copy(item, block).wait_send()
    ids = meta_ref[pl.ds(0, top), :]
    total = jnp.zeros((top, tokens), jnp.float32)
    for e in range(experts):
        total += jnp.where(ids == float(e), came_back[e], 0.0)
    gate_out[...] = total


def relayed(grad_out, expert_ids, gate_weights, down_weight, hidden_saved):
    experts = lax.axis_size("expert")
    tokens, width = grad_out.shape[1:]
    most, hidden_width = hidden_saved.shape[3:]
    top = expert_ids.shape[2]
    parts = column_parts(width)
    f32, bf16 = jnp.float32, jnp.bfloat16
    dma = pltpu.SemaphoreType.DMA
    vmem, any_space = pl.BlockSpec(memory_space=pltpu.VMEM), pl.BlockSpec(memory_space=pl.ANY)
    hidden_grad, gate_rows = pl.pallas_call(
        functools.partial(relay_kernel, most, parts),
        out_shape=(
            jax.ShapeDtypeStruct((experts, most, hidden_width), bf16),
            jax.ShapeDtypeStruct((top, tokens), f32),
        ),
        in_specs=[vmem, vmem, vmem, any_space, any_space],
        out_specs=(any_space, vmem),
        scratch_shapes=[
            pltpu.VMEM((experts, tokens, width), bf16),
            pltpu.VMEM((2 * top, tokens), f32),
            pltpu.VMEM((experts, 2 * top, tokens), f32),
            pltpu.VMEM((2 * top, tokens), f32),
            pltpu.VMEM((3, experts, 1, tokens), f32),
            pltpu.VMEM((hidden_width, width), bf16),
            pltpu.VMEM((experts, most, hidden_width), bf16),
            pltpu.VMEM((experts, most, hidden_width), bf16),
            pltpu.VMEM((experts, most, width), bf16),
            pltpu.VMEM((2, 8, most, max(size for _, _, size in parts)), bf16),
            pltpu.VMEM((BATCH * most, hidden_width), f32),
            pltpu.VMEM((experts, 8, tokens), f32),
            pltpu.VMEM((experts, 8, tokens), f32),
            dma((4,)),
            dma((len(parts) * experts * 4,)),
            dma((len(parts) * experts,)),
            dma((experts,)),
            dma((experts,)),
            dma((experts,)),
            dma((experts,)),
            dma((2 + experts,)),
        ],
        compiler_params=pltpu.CompilerParams(
            collective_id=0, has_side_effects=True, vmem_limit_bytes=56 * 1024 * 1024
        ),
        cost_estimate=pl.CostEstimate(
            flops=2 * experts * most * width * hidden_width, bytes_accessed=16 * 1024 * 1024, transcendentals=0
        ),
    )(grad_out[0], expert_ids[0].T, gate_weights[0].T, down_weight[0, 0], hidden_saved[0, 0])
    return hidden_grad[None, None], gate_rows.T[None]


def fits_relay(mesh):
    return mesh.shape["section"] == 2 and mesh.shape["expert"] == DEPTH * 4


def solution(mesh):
    in_specs = (
        P("section", "expert", None),
        P("section", "expert", None),
        P("section", "expert", None),
        P("section", "expert", None, None),
        P("section", "expert", None, None, None),
    )
    out_specs = (P("section", "expert", None, None, None), P("section", "expert", None))
    local_step = relayed if fits_relay(mesh) else gathered
    return jax.shard_map(local_step, mesh=mesh, in_specs=in_specs, out_specs=out_specs, check_vma=False)
```
